128 devices in a mesh: dp: 8 (over y_lo, x), tensor: 16 (over y_hi, z, core).
Axes of the slice: x: 4, y: 4 (y_hi: 2, y_lo: 2; y = y_hi * 2 + y_lo), z: 4, core: 2. Of those that a mesh axis runs over, the one named last changes fastest.
Arguments:
- tokens: bfloat16 [2048, 4096], P(('dp', 'tensor')), may hold values from -6 to 6
- rms_norm_gain: bfloat16 [4096], replicated, may hold values from 0.5 to 2
- w_gate: bfloat16 [4096, 14336], P(None, 'tensor'), may hold values from -0.09375 to 0.09375
- w_up: bfloat16 [4096, 14336], P(None, 'tensor'), may hold values from -0.09375 to 0.09375
- w_down: bfloat16 [14336, 4096], P('tensor'), may hold values from -0.046875 to 0.046875
- output_cotangent: bfloat16 [2048, 4096], P(('dp', 'tensor')), may hold values from -6 to 6
Outputs:
- layer_out: bfloat16 [2048, 4096], P(('dp', 'tensor'))
- token_input_gradient: bfloat16 [2048, 4096], P(('dp', 'tensor'))
- grad_gate: bfloat16 [4096, 14336], P('dp', 'tensor')
- grad_up: bfloat16 [4096, 14336], P('dp', 'tensor')
- grad_down: bfloat16 [14336, 4096], P('tensor', 'dp')
The draws below stay inside these ranges and needn't reach their ends.
All inputs are finite; a program needn't handle non-finite values.
Results may differ from the reference program's by a relative error of at most 0.019.
Values may be sent and summed in bfloat16 or wider, within the bound.
A program may use at most 192 MiB of HBM per device.

```python
import math
import jax
import jax.numpy as jnp
from jax import lax

D = 4096
FF = 14336
TOKENS = 2048
N_DP = 8


def steps_of(key, shape, cuts, smallest, high):
    def one(position, blocks):
        steps = jax.random.uniform(jax.random.fold_in(jax.random.fold_in(key, 6), position), (blocks,), jnp.float32, smallest / len(cuts), high / len(cuts))
        return jnp.repeat(jnp.exp(steps), shape[position] // blocks).reshape((-1,) + (1,) * (len(shape) - position - 1))

    factor_of = one(*cuts[0])
    for cut in cuts[1:]:
        factor_of = factor_of * one(*cut)
    return factor_of


def normal_values(own_key, extent, deviation, reach, split=(), held_as=jnp.bfloat16):
    level = steps_of(own_key, extent, split, -0.22, 0.18) if split else 1.0
    result = jax.random.normal(own_key, extent, jnp.float32) * deviation * level
    return jnp.minimum(jnp.maximum(result, -reach), reach).astype(held_as)


def setup_inputs(seed: int = 0) -> dict:
    keys = jax.random.split(jax.random.key(seed), 7)
    tokens = normal_values(keys[0], (TOKENS, D), 1.0, 6.0, ((0, 128),))
    rms_norm_gain = jnp.clip(jnp.exp(jax.random.uniform(keys[1], (D,), jnp.float32, math.log(0.5), math.log(2.0))), 0.5, 2.0).astype(jnp.bfloat16)
    w_gate = normal_values(keys[2], (D, FF), D ** -0.5, 0.09375, ((1, 16),))
    w_up = normal_values(keys[3], (D, FF), D ** -0.5, 0.09375, ((1, 16),))
    w_down = normal_values(keys[4], (FF, D), FF ** -0.5, 0.046875, ((0, 16),))
    output_cotangent = normal_values(keys[5], (TOKENS, D), 1.0, 6.0, ((0, 128),))
    return {"tokens": tokens, "rms_norm_gain": rms_norm_gain, "w_gate": w_gate, "w_up": w_up, "w_down": w_down, "output_cotangent": output_cotangent}


def reference(tokens, rms_norm_gain, w_gate, w_up, w_down, output_cotangent):
    input_float = tokens.astype(jnp.float32)
    reciprocal_scale = lax.rsqrt(lax.optimization_barrier(jnp.mean(input_float * input_float, axis=-1, keepdims=True)) + 1e-05)
    normalized_input = input_float * reciprocal_scale
    normalized_tokens = (normalized_input * rms_norm_gain.astype(jnp.float32)).astype(jnp.bfloat16)
    gate = jnp.dot(normalized_tokens, w_gate, preferred_element_type=jnp.float32)
    up = jnp.dot(normalized_tokens, w_up, preferred_element_type=jnp.float32)
    sig = jax.nn.sigmoid(gate)
    act = gate * sig
    hidden = (act * up).astype(jnp.bfloat16)
    layer_out = (input_float + jnp.dot(hidden, w_down, preferred_element_type=jnp.float32)).astype(jnp.bfloat16)
    d_hidden = jnp.dot(output_cotangent, w_down.T, preferred_element_type=jnp.float32)
    d_gate = (d_hidden * up * sig * (1.0 + gate * (1.0 - sig))).astype(jnp.bfloat16)
    d_up = (d_hidden * act).astype(jnp.bfloat16)
    d_normed = jnp.dot(d_gate, w_gate.T, preferred_element_type=jnp.float32) + jnp.dot(d_up, w_up.T, preferred_element_type=jnp.float32)
    gain_scaled_gradient = d_normed * rms_norm_gain.astype(jnp.float32)
    inner_product_sum = lax.optimization_barrier(jnp.mean(gain_scaled_gradient * normalized_input, axis=-1, keepdims=True))
    token_input_gradient = (output_cotangent.astype(jnp.float32) + reciprocal_scale * (gain_scaled_gradient - normalized_input * inner_product_sum)).astype(jnp.bfloat16)
    width = tokens.shape[1]
    normed_r = normalized_tokens.reshape(N_DP, -1, width)
    dout_r = output_cotangent.reshape(N_DP, -1, width)
    dgate_r = d_gate.reshape(N_DP, normed_r.shape[1], -1)
    dup_r = d_up.reshape(N_DP, normed_r.shape[1], -1)
    hidden_r = hidden.reshape(N_DP, normed_r.shape[1], -1)

    def replica(carry, pieces):
        nrm, dg, du, hid, dou = pieces
        part_gate = jnp.dot(nrm.T, dg, preferred_element_type=jnp.float32).astype(jnp.bfloat16)
        part_up = jnp.dot(nrm.T, du, preferred_element_type=jnp.float32).astype(jnp.bfloat16)
        part_down = jnp.dot(hid.T, dou, preferred_element_type=jnp.float32).astype(jnp.bfloat16)
        return ((carry[0] + part_gate.astype(jnp.float32), carry[1] + part_up.astype(jnp.float32), carry[2] + part_down.astype(jnp.float32)), None)
    start = (jnp.zeros(w_gate.shape, jnp.float32), jnp.zeros(w_up.shape, jnp.float32), jnp.zeros(w_down.shape, jnp.float32))
    totals, _ = lax.scan(replica, start, (normed_r, dgate_r, dup_r, hidden_r, dout_r))
    return (layer_out, token_input_gradient, totals[0].astype(jnp.bfloat16), totals[1].astype(jnp.bfloat16), totals[2].astype(jnp.bfloat16))
```

```python
import jax
import jax.numpy as jnp
from jax import lax
from jax.experimental import pallas as pl
from jax.experimental.pallas import tpu as pltpu
from jax.sharding import PartitionSpec as P

BF = jnp.bfloat16
F32 = jnp.float32
ROWS = 16
REP = 256
D = 4096
FL = 896
SL = 1024
HALF = 512
NX = 4

K_NRM, K_COT, K_SL = 0, 11, 22
K_A2A = 33
K_HID, K_DUP, K_DGT = 36, 40, 44
K_OUT, K_DNM = 48, 53
K_Y = 58
N_SEM = 61


def dot(a, b):
    return jnp.dot(a, b, preferred_element_type=F32)


def dot_t(a, b):
    return lax.dot_general(a, b, (((1,), (1,)), ((), ())), preferred_element_type=F32)


def kernel(
    tok, gain, cot_in, wg_hbm, wu_hbm, wd_hbm,
    lo_out, tig_out, gg_out, gu_out, gd_out,
    wgu, wd, nrm, cot, sl, osl, gu32, dh32, hid, hid_t, dgu, nrm_t,
    lo_part, dn_part, lo_sib, dn_sib, lo_z, dn_z, lo_zs, dn_zs, lo_y, dn_y,
    pg_send, pu_send, pd_send, pg_recv, pu_recv, pd_recv,
    gg_v, gu_v, gd_v, lo_v, tig_v,
    ss, rs, wsem, osem,
):
    dp = lax.axis_index("dp")
    t = lax.axis_index("tensor")
    x = lax.rem(dp, 4)
    yl = lax.div(dp, 4)
    core = lax.rem(t, 2)
    z = lax.rem(lax.div(t, 2), 4)
    yh = lax.div(t, 8)
    z_r, z_l, z_o = lax.rem(z + 1, 4), lax.rem(z + 3, 4), lax.rem(z + 2, 4)
    x_r, x_l, x_o = lax.rem(x + 1, 4), lax.rem(x + 3, 4), lax.rem(x + 2, 4)
    xr, xl, xo = (yl * 4 + x_r, t), (yl * 4 + x_l, t), (yl * 4 + x_o, t)
    yp = ((1 - yl) * 4 + x, t)
    sib = (dp, yh * 8 + z * 2 + (1 - core))
    zr, zl, zo = ((dp, yh * 8 + q * 2 + core) for q in (z_r, z_l, z_o))
    yhp = (dp, (1 - yh) * 8 + z * 2 + core)
    peers = (xr, xl, xo, yp, sib, zr, zl, zo, yhp)

    weights = [
        pltpu.make_async_copy(wg_hbm, wgu.at[:, pl.ds(0, FL)], wsem.at[0]),
        pltpu.make_async_copy(wu_hbm, wgu.at[:, pl.ds(FL, FL)], wsem.at[1]),
        pltpu.make_async_copy(wd_hbm, wd, wsem.at[2]),
    ]
    for w in weights:
        w.start()

    barrier = pltpu.get_barrier_semaphore()
    for dev in peers:
        pl.semaphore_signal(barrier, inc=1, device_id=dev, device_id_type=pl.DeviceIdType.MESH)

    sent = []

    def remote(src, dst, k, dev):
        return pltpu.make_async_remote_copy(
            src_ref=src, dst_ref=dst, send_sem=ss.at[k], recv_sem=rs.at[k],
            device_id=dev, device_id_type=pl.DeviceIdType.MESH,
        )

    def send(src, dst, k, dev):
        copy = remote(src, dst, k, dev)
        copy.start()
        sent.append(copy)

    def got(dst, k):
        remote(dst, dst, k, sib).wait_recv()

    def row(c, zz, y, n=ROWS):
        return pl.multiple_of((c * 8 + zz * 2 + y) * ROWS, n)

    def gather(view, k):
        def put(v, i, dev):
            send(v, v, k + i, dev)

        def s1():
            own = view(row(core, z, yh), ROWS)
            put(own, 0, yhp)
            put(own, 1, zr)
            put(own, 2, zl)

        def s2():
            other = view(row(core, z, 1 - yh), ROWS)
            got(other, k)
            put(other, 3, zr)
            put(other, 4, zl)
            put(view(row(core, z, 0, 32), 32), 5, sib)

        def s3():
            got(view(row(core, z_l, yh), ROWS), k + 1)
            got(view(row(core, z_l, 1 - yh), ROWS), k + 3)
            put(view(row(core, z_l, 0), ROWS), 6, zr)
            put(view(row(core, z_l, 0, 32), 32), 7, sib)
            got(view(row(core, z_r, yh), ROWS), k + 2)
            got(view(row(core, z_r, 1 - yh), ROWS), k + 4)
            put(view(row(core, z_r, 1), ROWS), 8, zl)
            put(view(row(core, z_r, 0, 32), 32), 9, sib)

        def s4():
            got(view(row(core, z_o, 0), ROWS), k + 6)
            got(view(row(core, z_o, 1), ROWS), k + 8)
            put(view(row(core, z_o, 0, 32), 32), 10, sib)

        def s5():
            for i, q in ((5, z), (7, z_l), (9, z_r), (10, z_o)):
                got(view(row(1 - core, q, 0, 32), 32), k + i)

        return s1, s2, s3, s4, s5

    n1, n2, n3, n4, n5 = gather(lambda r, n: nrm.at[pl.ds(r, n), :], K_NRM)
    c1, c2, c3, c4, c5 = gather(lambda r, n: cot.at[pl.ds(r, n), :], K_COT)
    s1, s2, s3, s4, s5 = gather(
        lambda r, n: sl.at[pl.ds(1, 3), :, pl.ds(r, n), :], K_SL
    )

    def along_x(block, half, k):
        def a1():
            send(block(0), block(3), k, xr)
            send(block(0), block(1), k + 1, xl)

        def a2():
            got(block(3), k)
            send(half(3, 0), half(2, 0), k + 2, xr)
            got(block(1), k + 1)
            send(half(1, 1), half(2, 1), k + 3, xl)

        def a3():
            got(half(2, 0), k + 2)
            got(half(2, 1), k + 3)

        return a1, a2, a3

    h1, h2, h3 = along_x(
        lambda s: hid_t.at[:, pl.ds(s * REP, REP)],
        lambda s, i: hid_t.at[pl.ds(i * (FL // 2), FL // 2), pl.ds(s * REP, REP)],
        K_HID,
    )

    def gate_side(at, k):
        return along_x(
            lambda s: dgu.at[pl.ds(s * REP, REP), pl.ds(at, FL)],
            lambda s, i: dgu.at[pl.ds(s * REP + i * 128, 128), pl.ds(at, FL)],
            k,
        )

    u1, u2, u3 = gate_side(FL, K_DUP)
    g1, g2, g3 = gate_side(0, K_DGT)

    def reduce(part, by_core, by_z, z_sum, by_y, k):
        def r1():
            send(part.at[pl.ds(pl.multiple_of((1 - core) * 128, 128), 128), :], by_core, k, sib)

        def r2():
            got(by_core, k)
            base = core * 128

            @pl.loop(0, 4)
            def _(i):
                at = pl.ds(pl.multiple_of(base + i * 32, 32), 32)
                part[at, :] = (
                    part[at, :].astype(F32)
                    + by_core[pl.ds(pl.multiple_of(i * 32, 32), 32), :].astype(F32)
                ).astype(BF)

            for i, (q, dev) in enumerate(((z_r, zr), (z_l, zl), (z_o, zo))):
                at = pl.ds(pl.multiple_of(base + q * 32, 32), 32)
                send(part.at[at, :], by_z.at[i], k + 1 + i, dev)

        def r3():
            for i in range(3):
                got(by_z.at[i], k + 1 + i)
            at = pl.ds(pl.multiple_of(core * 128 + z * 32, 32), 32)
            z_sum[...] = (
                part[at, :].astype(F32)
                + by_z[0].astype(F32)
                + by_z[1].astype(F32)
                + by_z[2].astype(F32)
            ).astype(BF)
            send(z_sum.at[pl.ds(pl.multiple_of((1 - yh) * ROWS, ROWS), ROWS), :], by_y, k + 4, yhp)

        def r4():
            got(by_y, k + 4)
            own = z_sum[pl.ds(pl.multiple_of(yh * ROWS, ROWS), ROWS), :]
            return own.astype(F32) + by_y[...].astype(F32)

        return r1, r2, r3, r4

    o1, o2, o3, o4 = reduce(lo_part, lo_sib, lo_z, lo_zs, lo_y, K_OUT)
    d1, d2, d3, d4 = reduce(dn_part, dn_sib, dn_z, dn_zs, dn_y, K_DNM)

    own = pl.ds(row(core, z, yh), ROWS)
    tokens = tok[...].astype(F32)
    rscale = lax.rsqrt(jnp.mean(tokens * tokens, axis=-1, keepdims=True) + 1e-5)
    gains = gain[...].astype(F32)
    normed = (tokens * rscale * gains).astype(BF)
    nrm[own, :] = normed
    cot[own, :] = cot_in[...]

    pl.semaphore_wait(barrier, len(peers))
    n1()
    c1()
    for q in range(NX):
        for j in range(2):
            lanes = pl.ds(j * 2048 + q * HALF, HALF)
            osl[q, 0, :, pl.ds(j * HALF, HALF)] = nrm[own, lanes]
            osl[q, 1, :, pl.ds(j * HALF, HALF)] = cot_in[:, lanes]
    for i, (q, dev, slot) in enumerate(((x_r, xr, 3), (x_l, xl, 1), (x_o, xo, 2))):
        send(osl.at[q], sl.at[slot, :, own, :], K_A2A + i, dev)

    n2()
    c2()
    n3()
    c3()
    n4()
    for i, slot in enumerate((3, 1, 2)):
        got(sl.at[slot, :, own, :], K_A2A + i)
    n5()
    weights[0].wait()
    weights[1].wait()

    def gate_up(i):
        at = pl.ds(pl.multiple_of(i * 256, 256), 256)
        gu32[:, at] = dot(nrm[...], wgu[:, at])

    pl.loop(0, 3)(gate_up)
    c4()
    s1()
    pl.loop(3, 7)(gate_up)

    @pl.loop(0, REP // 32)
    def _(i):
        at = pl.ds(pl.multiple_of(i * 32, 32), 32)
        gate, up = gu32[at, pl.ds(0, FL)], gu32[at, pl.ds(FL, FL)]
        hid[at, :] = (gate * jax.nn.sigmoid(gate) * up).astype(BF)

    hid_t[:, pl.ds(0, REP)] = hid[...].T
    h1()
    s2()
    c5()
    weights[2].wait()

    @pl.loop(0, 3)
    def _(i):
        at = pl.ds(pl.multiple_of(i * 256, 256), 256)
        dh32[:, at] = dot_t(cot[...], wd[at, :])

    dh32[:, pl.ds(768, 128)] = dot_t(cot[...], wd[pl.ds(768, 128), :])

    @pl.loop(0, REP // 32)
    def _(i):
        at = pl.ds(pl.multiple_of(i * 32, 32), 32)
        gate, up = gu32[at, pl.ds(0, FL)], gu32[at, pl.ds(FL, FL)]
        dh = dh32[at, :]
        sig = jax.nn.sigmoid(gate)
        dgu[at, pl.ds(0, FL)] = (dh * up * sig * (1.0 + gate * (1.0 - sig))).astype(BF)
        dgu[at, pl.ds(FL, FL)] = (dh * (gate * sig)).astype(BF)

    u1()
    g1()
    s3()
    h2()

    @pl.loop(0, D // 512)
    def _(i):
        at = pl.ds(pl.multiple_of(i * 512, 512), 512)
        lo_part[:, at] = dot(hid[...], wd[:, at]).astype(BF)

    o1()
    s4()

    @pl.loop(0, D // 512)
    def _(i):
        at = pl.ds(pl.multiple_of(i * 512, 512), 512)
        dn_part[:, at] = dot_t(dgu[pl.ds(0, REP), :], wgu[at, :]).astype(BF)

    d1()
    u2()
    o2()
    g2()
    for j in range(2):
        lanes = pl.ds(pl.multiple_of(j * 2048 + x * HALF, HALF), HALF)
        sl[0, 0, :, pl.ds(j * HALF, HALF)] = nrm[:, lanes]
        sl[0, 1, :, pl.ds(j * HALF, HALF)] = cot[:, lanes]
    s5()

    @pl.loop(0, NX)
    def _(r):
        nrm_t[:, pl.ds(pl.multiple_of(r * REP, REP), REP)] = sl[r, 0].T

    d2()
    o3()

    def halves(which):
        return pl.ds(pl.multiple_of(which * HALF, HALF), HALF)

    def grad_down(which):
        acc = None
        for r in range(NX):
            p = dot(hid_t[:, pl.ds(r * REP, REP)], sl[r, 1, :, halves(which)])
            acc = p if acc is None else acc + p
        return acc.astype(BF)

    def grad_side(which, at):
        return dot(nrm_t[halves(which), :], dgu[:, pl.ds(at, FL)]).astype(BF)

    h3()
    pd_send[...] = grad_down(1 - yl)
    send(pd_send, pd_recv, K_Y, yp)
    u3()
    pu_send[...] = grad_side(1 - yl, FL)
    send(pu_send, pu_recv, K_Y + 1, yp)
    d3()
    g3()
    pg_send[...] = grad_side(1 - yl, 0)
    send(pg_send, pg_recv, K_Y + 2, yp)
    gd_v[...] = grad_down(yl)
    gu_v[...] = grad_side(yl, FL)
    gg_v[...] = grad_side(yl, 0)

    out = []

    def leave(v, o, i):
        copy = pltpu.make_async_copy(v, o, osem.at[i])
        copy.start()
        out.append(copy)

    lo_v[...] = (tokens + o4()).astype(BF)
    leave(lo_v, lo_out, 0)
    g = d4() * gains
    xhat = tokens * rscale
    inner = jnp.mean(g * xhat, axis=-1, keepdims=True)
    tig_v[...] = (cot_in[...].astype(F32) + rscale * (g - xhat * inner)).astype(BF)
    leave(tig_v, tig_out, 1)

    for i, (v, recv, o) in enumerate(
        ((gd_v, pd_recv, gd_out), (gu_v, pu_recv, gu_out), (gg_v, pg_recv, gg_out))
    ):
        got(recv, K_Y + i)
        v[...] = (v[...].astype(F32) + recv[...].astype(F32)).astype(BF)
        leave(v, o, 2 + i)
    for copy in sent:
        copy.wait_send()
    for copy in out:
        copy.wait()


def local(tokens, rms_norm_gain, w_gate, w_up, w_down, output_cotangent):
    vmem = pl.BlockSpec(memory_space=pltpu.VMEM)
    hbm = pl.BlockSpec(memory_space=pl.ANY)

    def bf(*shape):
        return pltpu.VMEM(shape, BF)

    call = pl.pallas_call(
        kernel,
        out_shape=[
            jax.ShapeDtypeStruct((ROWS, D), BF),
            jax.ShapeDtypeStruct((ROWS, D), BF),
            jax.ShapeDtypeStruct((HALF, FL), BF),
            jax.ShapeDtypeStruct((HALF, FL), BF),
            jax.ShapeDtypeStruct((FL, HALF), BF),
        ],
        in_specs=[vmem, vmem, vmem, hbm, hbm, hbm],
        out_specs=[hbm] * 5,
        scratch_shapes=[
            bf(D, 2 * FL), bf(FL, D), bf(REP, D), bf(REP, D),
            bf(NX, 2, REP, SL), bf(NX, 2, ROWS, SL),
            pltpu.VMEM((REP, 2 * FL), F32), pltpu.VMEM((REP, FL), F32),
            bf(REP, FL), bf(FL, NX * REP), bf(NX * REP, 2 * FL), bf(SL, NX * REP),
            bf(REP, D), bf(REP, D), bf(128, D), bf(128, D),
            bf(3, 32, D), bf(3, 32, D), bf(32, D), bf(32, D), bf(ROWS, D), bf(ROWS, D),
            bf(HALF, FL), bf(HALF, FL), bf(FL, HALF),
            bf(HALF, FL), bf(HALF, FL), bf(FL, HALF),
            bf(HALF, FL), bf(HALF, FL), bf(FL, HALF),
            bf(ROWS, D), bf(ROWS, D),
            pltpu.SemaphoreType.DMA((N_SEM,)),
            pltpu.SemaphoreType.DMA((N_SEM,)),
            pltpu.SemaphoreType.DMA((3,)),
            pltpu.SemaphoreType.DMA((5,)),
        ],
        compiler_params=pltpu.CompilerParams(
            collective_id=0, has_side_effects=True, vmem_limit_bytes=63 * 1000 * 1000
        ),
        cost_estimate=pl.CostEstimate(
            flops=18 * REP * D * FL, bytes_accessed=6 * D * FL, transcendentals=2 * REP * FL
        ),
    )
    return tuple(
        call(tokens, rms_norm_gain.reshape(1, D), output_cotangent, w_gate, w_up, w_down)
    )


def solution(mesh):
    placed = (
        P(("dp", "tensor"), None),
        P(),
        P(None, "tensor"),
        P(None, "tensor"),
        P("tensor", None),
        P(("dp", "tensor"), None),
    )
    return jax.shard_map(
        local,
        mesh=mesh,
        in_specs=placed,
        out_specs=(
            P(("dp", "tensor"), None),
            P(("dp", "tensor"), None),
            P("dp", "tensor"),
            P("dp", "tensor"),
            P("tensor", "dp"),
        ),
        check_vma=False,
    )
```

```python
import jax
import jax.numpy as jnp
from jax import lax
from jax.experimental import pallas as pl
from jax.experimental.pallas import tpu as pltpu
from jax.sharding import PartitionSpec as P

BF = jnp.bfloat16
F32 = jnp.float32
ROWS = 16
REP = 256
D = 4096
FL = 896
SL = 1024
HALF = 512
NX = 4

K_NRM, K_COT, K_SLN, K_SLC = 0, 13, 26, 39
K_CUT, K_A2A = 52, 53
K_HA, K_HB, K_PA, K_PB = 56, 60, 64, 68
K_UA, K_UB, K_GA, K_GB = 72, 76, 80, 84
K_OUT, K_DNM = 88, 93
K_HY, K_YUA, K_YUB, K_YGA, K_YGB = 98, 99, 100, 101, 102
N_SEM = 103
WA, WB = 512, 384


def dot(a, b):
    return jnp.dot(a, b, preferred_element_type=F32)


def dot_t(a, b):
    return lax.dot_general(a, b, (((1,), (1,)), ((), ())), preferred_element_type=F32)


def kernel(
    tok, gain, cot_in, wg_hbm, wu_hbm, wd_hbm,
    lo_out, tig_out, gg_out, gu_out, gd_out,
    wgu, wd, nrm, cot, sl, osl, cut, gu32, hid, hid_t, dgu, nrm_t,
    lo_part, dn_part, lo_sib, dn_sib, lo_z, dn_z, lo_zs, dn_zs, lo_y, dn_y,
    pg_send, pu_send, pg_recv, pu_recv,
    gg_v, gu_v, gd_v, lo_v, tig_v,
    ss, rs, wsem, osem,
):
    dp = lax.axis_index("dp")
    t = lax.axis_index("tensor")
    x = lax.rem(dp, 4)
    yl = lax.div(dp, 4)
    core = lax.rem(t, 2)
    z = lax.rem(lax.div(t, 2), 4)
    yh = lax.div(t, 8)
    z_r, z_l, z_o = lax.rem(z + 1, 4), lax.rem(z + 3, 4), lax.rem(z + 2, 4)
    x_r, x_l, x_o = lax.rem(x + 1, 4), lax.rem(x + 3, 4), lax.rem(x + 2, 4)
    xr, xl, xo = (yl * 4 + x_r, t), (yl * 4 + x_l, t), (yl * 4 + x_o, t)
    yp = ((1 - yl) * 4 + x, t)
    sib = (dp, yh * 8 + z * 2 + (1 - core))
    zr, zl, zo = ((dp, yh * 8 + q * 2 + core) for q in (z_r, z_l, z_o))
    yhp = (dp, (1 - yh) * 8 + z * 2 + core)
    peers = (xr, xl, xo, yp, sib, zr, zl, zo, yhp)

    weights = [
        pltpu.make_async_copy(wg_hbm, wgu.at[:, pl.ds(0, FL)], wsem.at[0]),
        pltpu.make_async_copy(wu_hbm, wgu.at[:, pl.ds(FL, FL)], wsem.at[1]),
        pltpu.make_async_copy(wd_hbm, wd, wsem.at[2]),
    ]
    for w in weights:
        w.start()

    barrier = pltpu.get_barrier_semaphore()
    for dev in peers:
        pl.semaphore_signal(barrier, inc=1, device_id=dev, device_id_type=pl.DeviceIdType.MESH)

    sent = []

    def remote(src, dst, k, dev):
        return pltpu.make_async_remote_copy(
            src_ref=src, dst_ref=dst, send_sem=ss.at[k], recv_sem=rs.at[k],
            device_id=dev, device_id_type=pl.DeviceIdType.MESH,
        )

    def send(src, dst, k, dev):
        copy = remote(src, dst, k, dev)
        copy.start()
        sent.append(copy)

    def got(dst, k):
        remote(dst, dst, k, sib).wait_recv()

    def row(c, zz, y, n=ROWS):
        return pl.multiple_of((c * 8 + zz * 2 + y) * ROWS, n)

    def gather(view, part, k):
        def put(v, i, dev):
            send(v, v, k + i, dev)

        def s1y():
            put(view(row(core, z, yh), ROWS), 0, yhp)

        def s1z():
            own = view(row(core, z, yh), ROWS)
            put(own, 1, zr)
            put(own, 2, zl)

        def s2():
            got(view(row(core, z_l, yh), ROWS), k + 1)
            put(part(row(core, z_l, yh), 0), 3, zr)
            got(view(row(core, z_r, yh), ROWS), k + 2)
            put(part(row(core, z_r, yh), 1), 4, zl)

        def s3():
            other = view(row(core, z, 1 - yh), ROWS)
            got(other, k)
            put(other, 5, zr)
            put(other, 6, zl)
            put(view(row(core, z, 0, 32), 32), 7, sib)

        def s4():
            got(view(row(core, z_l, 1 - yh), ROWS), k + 5)
            put(part(row(core, z_l, 1 - yh), 0), 8, zr)
            got(view(row(core, z_r, 1 - yh), ROWS), k + 6)
            put(part(row(core, z_r, 1 - yh), 1), 9, zl)
            put(view(row(core, z_l, 0, 32), 32), 10, sib)
            put(view(row(core, z_r, 0, 32), 32), 11, sib)

        def s5():
            got(part(row(core, z_o, yh), 0), k + 3)
            got(part(row(core, z_o, yh), 1), k + 4)
            got(part(row(core, z_o, 1 - yh), 0), k + 8)
            got(part(row(core, z_o, 1 - yh), 1), k + 9)
            put(view(row(core, z_o, 0, 32), 32), 12, sib)

        def s6():
            for i, q in ((7, z), (10, z_l), (11, z_r), (12, z_o)):
                got(view(row(1 - core, q, 0, 32), 32), k + i)

        return s1y, s1z, s2, s3, s4, s5, s6

    def rows_gather(ref, k):
        return gather(
            lambda r, n: ref.at[pl.ds(r, n), :],
            lambda r, i: ref.at[pl.ds(r, ROWS), pl.ds(i * 2048, 2048)],
            k,
        )

    n1y, n1z, n2, n3, n4, n5, n6 = rows_gather(nrm, K_NRM)
    c1y, c1z, c2, c3, c4, c5, c6 = rows_gather(cot, K_COT)
    a1y, a1z, a2, a3, a4, a5, a6 = gather(
        lambda r, n: sl.at[pl.ds(0, 2), pl.ds(1, 3), pl.ds(r, n), :],
        lambda r, i: sl.at[pl.ds(i, 1), pl.ds(1, 3), pl.ds(r, ROWS), :],
        K_SLN,
    )
    b1y, b1z, b2, b3, b4, b5, b6 = gather(
        lambda r, n: sl.at[pl.ds(2, 2), :, pl.ds(r, n), :],
        lambda r, i: sl.at[pl.ds(2 + i, 1), :, pl.ds(r, ROWS), :],
        K_SLC,
    )

    def along_x(block, half, k):
        def x1():
            send(block(0), block(3), k, xr)
            send(block(0), block(1), k + 1, xl)

        def x2():
            got(block(3), k)
            send(half(3, 0), half(2, 0), k + 2, xr)
            got(block(1), k + 1)
            send(half(1, 1), half(2, 1), k + 3, xl)

        def x3():
            got(half(2, 0), k + 2)
            got(half(2, 1), k + 3)

        return x1, x2, x3

    def hidden_side(plane, at, k):
        def lanes(s):
            return pl.ds((plane * NX + s) * REP, REP)

        return along_x(
            lambda s: hid_t.at[pl.ds(at, 448), lanes(s)],
            lambda s, i: hid_t.at[pl.ds(at + i * 224, 224), lanes(s)],
            k,
        )

    def gate_side(at, n, k):
        return along_x(
            lambda s: dgu.at[pl.ds(s * REP, REP), pl.ds(at, n)],
            lambda s, i: dgu.at[pl.ds(s * REP + i * 128, 128), pl.ds(at, n)],
            k,
        )

    ha1, ha2, ha3 = hidden_side(0, 0, K_HA)
    hb1, hb2, hb3 = hidden_side(0, 448, K_HB)
    pa1, pa2, pa3 = hidden_side(1, 0, K_PA)
    pb1, pb2, pb3 = hidden_side(1, 448, K_PB)
    ua1, ua2, ua3 = gate_side(FL, WA, K_UA)
    ub1, ub2, ub3 = gate_side(FL + WA, WB, K_UB)
    ga1, ga2, ga3 = gate_side(0, WA, K_GA)
    gb1, gb2, gb3 = gate_side(WA, WB, K_GB)

    def reduce(part, by_core, by_z, z_sum, by_y, k):
        def r1():
            send(part.at[pl.ds(pl.multiple_of((1 - core) * 128, 128), 128), :], by_core, k, sib)

        def r2():
            got(by_core, k)
            base = core * 128

            @pl.loop(0, 4)
            def _(i):
                at = pl.ds(pl.multiple_of(base + i * 32, 32), 32)
                part[at, :] = (
                    part[at, :].astype(F32)
                    + by_core[pl.ds(pl.multiple_of(i * 32, 32), 32), :].astype(F32)
                ).astype(BF)

            for i, (q, dev) in enumerate(((z_r, zr), (z_l, zl), (z_o, zo))):
                at = pl.ds(pl.multiple_of(base + q * 32, 32), 32)
                send(part.at[at, :], by_z.at[i], k + 1 + i, dev)

        def r3():
            for i in range(3):
                got(by_z.at[i], k + 1 + i)
            at = pl.ds(pl.multiple_of(core * 128 + z * 32, 32), 32)
            z_sum[...] = (
                part[at, :].astype(F32)
                + by_z[0].astype(F32)
                + by_z[1].astype(F32)
                + by_z[2].astype(F32)
            ).astype(BF)
            send(z_sum.at[pl.ds(pl.multiple_of((1 - yh) * ROWS, ROWS), ROWS), :], by_y, k + 4, yhp)

        def r4():
            got(by_y, k + 4)
            own = z_sum[pl.ds(pl.multiple_of(yh * ROWS, ROWS), ROWS), :]
            return own.astype(F32) + by_y[...].astype(F32)

        return r1, r2, r3, r4

    o1, o2, o3, o4 = reduce(lo_part, lo_sib, lo_z, lo_zs, lo_y, K_OUT)
    d1, d2, d3, d4 = reduce(dn_part, dn_sib, dn_z, dn_zs, dn_y, K_DNM)

    own = pl.ds(row(core, z, yh), ROWS)
    tokens = tok[...].astype(F32)
    rscale = lax.rsqrt(jnp.mean(tokens * tokens, axis=-1, keepdims=True) + 1e-5)
    gains = gain[...].reshape(1, D).astype(F32)
    nrm[own, :] = (tokens * rscale * gains).astype(BF)
    cot[own, :] = cot_in[...]

    pl.semaphore_wait(barrier, len(peers))
    n1y()
    n1z()
    send(cot_in.at[:, pl.ds(pl.multiple_of((1 - yl) * 2048, 2048), 2048)], cut, K_CUT, yp)
    c1y()
    for q in range(NX):
        osl[q, 0] = nrm[own, pl.ds(q * HALF, HALF)]
        osl[q, 1] = nrm[own, pl.ds(2048 + q * HALF, HALF)]
        osl[q, 2] = cot_in[:, pl.ds(pl.multiple_of(yl * 2048 + q * HALF, HALF), HALF)]
    n2()
    n3()
    c1z()
    got(cut, K_CUT)
    for q in range(NX):
        osl[q, 3] = cut[:, pl.ds(q * HALF, HALF)]
    for i, (q, dev, slot) in enumerate(((x_r, xr, 3), (x_l, xl, 1), (x_o, xo, 2))):
        send(osl.at[q], sl.at[:, slot, own, :], K_A2A + i, dev)
    for i in range(2, 4):
        sl[i, 0, own, :] = osl[x, i]
    n4()
    c2()
    c3()
    n5()
    for i, slot in enumerate((3, 1, 2)):
        got(sl.at[:, slot, own, :], K_A2A + i)
    a1y()
    weights[0].wait()
    weights[1].wait()
    n6()

    def gate_up(i):
        at = pl.ds(pl.multiple_of(i * 256, 256), 256)
        gu32[:, at] = dot(nrm[...], wgu[:, at])

    pl.loop(0, 2)(gate_up)
    c4()
    a1z()
    b1y()
    pl.loop(2, 5)(gate_up)
    c5()
    a2()
    a3()
    pl.loop(5, 7)(gate_up)

    @pl.loop(0, REP // 32)
    def _(i):
        at = pl.ds(pl.multiple_of(i * 32, 32), 32)
        gate, up = gu32[at, pl.ds(0, FL)], gu32[at, pl.ds(FL, FL)]
        hid[at, :] = (gate * jax.nn.sigmoid(gate) * up).astype(BF)

    hid_t[:, pl.ds(0, REP)] = hid[...].T
    send(hid_t.at[:, pl.ds(0, REP)], hid_t.at[:, pl.ds(NX * REP, REP)], K_HY, yp)
    ha1()
    c6()
    weights[2].wait()

    def gate_grads(at, n):
        dh = dot_t(cot[...], wd[pl.ds(at, n), :])
        gate, up = gu32[:, pl.ds(at, n)], gu32[:, pl.ds(pl.multiple_of(FL + at, 128), n)]
        sig = jax.nn.sigmoid(gate)
        dgu[pl.ds(0, REP), pl.ds(at, n)] = (
            dh * up * sig * (1.0 + gate * (1.0 - sig))
        ).astype(BF)
        dgu[pl.ds(0, REP), pl.ds(pl.multiple_of(FL + at, 128), n)] = (dh * (gate * sig)).astype(BF)

    @pl.loop(0, 3)
    def _(i):
        gate_grads(pl.multiple_of(i * 256, 256), 256)

    gate_grads(768, 128)
    ua1()
    ub1()

    def layer_tile(i):
        at = pl.ds(pl.multiple_of(i * 512, 512), 512)
        lo_part[:, at] = dot(hid[...], wd[:, at]).astype(BF)

    def normed_tile(i):
        at = pl.ds(pl.multiple_of(i * 512, 512), 512)
        dn_part[:, at] = dot_t(dgu[pl.ds(0, REP), :], wgu[at, :]).astype(BF)

    a4()
    ha2()
    pl.loop(0, 8)(layer_tile)
    o1()
    a5()
    b1z()
    pl.loop(0, 4)(normed_tile)
    ua2()
    ga1()
    o2()
    a6()

    for j in range(2):
        lanes = pl.ds(pl.multiple_of(j * 2048 + x * HALF, HALF), HALF)
        nrm_t[pl.ds(j * HALF, HALF), pl.ds(0, REP)] = nrm[:, lanes].T

    @pl.loop(1, NX)
    def _(r):
        at = pl.ds(pl.multiple_of(r * REP, REP), REP)
        nrm_t[pl.ds(0, HALF), at] = sl[0, r].T
        nrm_t[pl.ds(HALF, HALF), at] = sl[1, r].T

    ub2()
    gb1()

    def halves(which):
        return pl.ds(pl.multiple_of(which * HALF, HALF), HALF)

    def side(which, at, n):
        return dot(nrm_t[halves(which), :], dgu[:, pl.ds(at, n)]).astype(BF)

    ua3()
    pu_send[:, pl.ds(0, WA)] = side(1 - yl, FL, WA)
    send(pu_send.at[:, pl.ds(0, WA)], pu_recv.at[:, pl.ds(0, WA)], K_YUA, yp)
    b2()
    b3()
    ub3()
    pu_send[:, pl.ds(WA, WB)] = side(1 - yl, FL + WA, WB)
    send(pu_send.at[:, pl.ds(WA, WB)], pu_recv.at[:, pl.ds(WA, WB)], K_YUB, yp)
    got(hid_t.at[:, pl.ds(NX * REP, REP)], K_HY)
    hb1()
    pl.loop(4, 8)(normed_tile)
    d1()
    ga2()
    pa1()
    gu_v[...] = side(yl, FL, FL)
    gb2()
    pb1()
    b4()
    d2()
    ga3()
    pg_send[:, pl.ds(0, WA)] = side(1 - yl, 0, WA)
    send(pg_send.at[:, pl.ds(0, WA)], pg_recv.at[:, pl.ds(0, WA)], K_YGA, yp)
    gb3()
    pg_send[:, pl.ds(WA, WB)] = side(1 - yl, WA, WB)
    send(pg_send.at[:, pl.ds(WA, WB)], pg_recv.at[:, pl.ds(WA, WB)], K_YGB, yp)
    hb2()
    o3()
    b5()
    gg_v[...] = side(yl, 0, FL)
    pa2()
    d3()
    b6()

    def down(plane):
        return dot(
            hid_t[:, pl.ds(plane * NX * REP, NX * REP)],
            sl[2 + plane].reshape(NX * REP, HALF),
        )

    ha3()
    hb3()
    gd_v[...] = down(0).astype(BF)
    pb2()

    out = []

    def leave(v, o, i):
        copy = pltpu.make_async_copy(v, o, osem.at[i])
        copy.start()
        out.append(copy)

    lo_v[...] = (tokens + o4()).astype(BF)
    leave(lo_v, lo_out, 0)
    g = d4() * gains
    xhat = tokens * rscale
    inner = jnp.mean(g * xhat, axis=-1, keepdims=True)
    tig_v[...] = (cot_in[...].astype(F32) + rscale * (g - xhat * inner)).astype(BF)
    leave(tig_v, tig_out, 1)

    def finish(v, recv, at, n, k):
        lanes = pl.ds(at, n)
        got(recv.at[:, lanes], k)
        v[:, lanes] = (v[:, lanes].astype(F32) + recv[:, lanes].astype(F32)).astype(BF)

    finish(gu_v, pu_recv, 0, WA, K_YUA)
    finish(gu_v, pu_recv, WA, WB, K_YUB)
    leave(gu_v, gu_out, 2)
    finish(gg_v, pg_recv, 0, WA, K_YGA)
    pa3()
    pb3()
    gd_v[...] = (gd_v[...].astype(F32) + down(1)).astype(BF)
    leave(gd_v, gd_out, 3)
    finish(gg_v, pg_recv, WA, WB, K_YGB)
    leave(gg_v, gg_out, 4)
    for copy in sent:
        copy.wait_send()
    for copy in out:
        copy.wait()


def move(*refs):
    sources, results, held = refs[:5], refs[5:10], refs[10:15]
    sems_in, sems_out = refs[15:]
    ins = [pltpu.make_async_copy(a, v, sems_in.at[i]) for i, (a, v) in enumerate(zip(sources, held))]
    outs = [pltpu.make_async_copy(v, b, sems_out.at[i]) for i, (v, b) in enumerate(zip(held, results))]
    for copy in ins:
        copy.start()
    for arrived, copy in zip(ins, outs):
        arrived.wait()
        copy.start()
    for copy in outs:
        copy.wait()


def local(tokens, rms_norm_gain, w_gate, w_up, w_down, output_cotangent):
    vmem = pl.BlockSpec(memory_space=pltpu.VMEM)
    hbm = pl.BlockSpec(memory_space=pl.ANY)

    def bf(*shape):
        return pltpu.VMEM(shape, BF)

    shapes = [
        jax.ShapeDtypeStruct((ROWS, D), BF),
        jax.ShapeDtypeStruct((ROWS, D), BF),
        jax.ShapeDtypeStruct((HALF, FL), BF),
        jax.ShapeDtypeStruct((HALF, FL), BF),
        jax.ShapeDtypeStruct((FL, HALF), BF),
    ]
    call = pl.pallas_call(
        kernel,
        out_shape=shapes,
        in_specs=[vmem, vmem, vmem, hbm, hbm, hbm],
        out_specs=[hbm] * 5,
        scratch_shapes=[
            bf(D, 2 * FL), bf(FL, D), bf(REP, D), bf(REP, D),
            bf(4, NX, REP, HALF), bf(NX, 4, ROWS, HALF), bf(ROWS, 2048),
            pltpu.VMEM((REP, 2 * FL), F32),
            bf(REP, FL), bf(FL, 2 * NX * REP), bf(NX * REP, 2 * FL), bf(SL, NX * REP),
            bf(REP, D), bf(REP, D), bf(128, D), bf(128, D),
            bf(3, 32, D), bf(3, 32, D), bf(32, D), bf(32, D), bf(ROWS, D), bf(ROWS, D),
            bf(HALF, FL), bf(HALF, FL), bf(HALF, FL), bf(HALF, FL),
            bf(HALF, FL), bf(HALF, FL), bf(FL, HALF),
            bf(ROWS, D), bf(ROWS, D),
            pltpu.SemaphoreType.DMA((N_SEM,)),
            pltpu.SemaphoreType.DMA((N_SEM,)),
            pltpu.SemaphoreType.DMA((3,)),
            pltpu.SemaphoreType.DMA((5,)),
        ],
        compiler_params=pltpu.CompilerParams(
            collective_id=0, has_side_effects=True, vmem_limit_bytes=63 * 1000 * 1000
        ),
        cost_estimate=pl.CostEstimate(
            flops=18 * REP * D * FL, bytes_accessed=6 * D * FL, transcendentals=2 * REP * FL
        ),
    )
    results = call(tokens, rms_norm_gain, output_cotangent, w_gate, w_up, w_down)
    moved = pl.pallas_call(
        move,
        out_shape=shapes,
        in_specs=[hbm] * 5,
        out_specs=[hbm] * 5,
        scratch_shapes=[pltpu.VMEM(a.shape, BF) for a in shapes]
        + [pltpu.SemaphoreType.DMA((5,)), pltpu.SemaphoreType.DMA((5,))],
    )(*results)
    return tuple(moved)


def solution(mesh):
    placed = (
        P(("dp", "tensor"), None),
        P(),
        P(None, "tensor"),
        P(None, "tensor"),
        P("tensor", None),
        P(("dp", "tensor"), None),
    )
    return jax.shard_map(
        local,
        mesh=mesh,
        in_specs=placed,
        out_specs=(
            P(("dp", "tensor"), None),
            P(("dp", "tensor"), None),
            P("dp", "tensor"),
            P("dp", "tensor"),
            P("tensor", "dp"),
        ),
        check_vma=False,
    )
```

```python
import jax
import jax.numpy as jnp
from jax import lax
from jax.experimental import pallas as pl
from jax.experimental.pallas import tpu as pltpu
from jax.sharding import PartitionSpec as P

BF = jnp.bfloat16
F32 = jnp.float32
ROWS = 16
REP = 256
D = 4096
FL = 896
SL = 1024
HALF = 512
NX = 4

K_NRM, K_COT, K_SLN, K_SLC = 0, 20, 40, 49
K_CUT, K_A2A = 58, 59
K_H1, K_H2, K_PA, K_PB = 62, 66, 70, 74
K_U1, K_UA, K_UB, K_G1, K_GA, K_GB = 78, 82, 86, 90, 94, 98
K_OUT, K_DNM = 102, 107
K_HY1, K_HY2, K_YUA, K_YUB, K_YGA, K_YGB = 112, 113, 114, 115, 116, 117
N_SEM = 118
GRP = 128
WA, WB = 512, 384


def dot(a, b):
    return jnp.dot(a, b, preferred_element_type=F32)


def dot_t(a, b):
    return lax.dot_general(a, b, (((1,), (1,)), ((), ())), preferred_element_type=F32)


def kernel(
    tok, gain, cot_in, wg_hbm, wu_hbm, wd_hbm,
    lo_out, tig_out, gg_out, gu_out, gd_out,
    wgu, wd, nrm, cot, sl, osl, cut, gu32, hid, hid_t, dgu, nrm_t,
    lo_part, dn_part, lo_sib, dn_sib, lo_z, dn_z, lo_zs, dn_zs, lo_y, dn_y,
    pg_send, pu_send, pg_recv, pu_recv,
    gg_v, gu_v, gd_v, lo_v, tig_v,
    ss, rs, wsem, osem,
):
    dp = lax.axis_index("dp")
    t = lax.axis_index("tensor")
    x = lax.rem(dp, 4)
    yl = lax.div(dp, 4)
    core = lax.rem(t, 2)
    z = lax.rem(lax.div(t, 2), 4)
    yh = lax.div(t, 8)
    z_r, z_l, z_o = lax.rem(z + 1, 4), lax.rem(z + 3, 4), lax.rem(z + 2, 4)
    x_r, x_l, x_o = lax.rem(x + 1, 4), lax.rem(x + 3, 4), lax.rem(x + 2, 4)
    xr, xl, xo = (yl * 4 + x_r, t), (yl * 4 + x_l, t), (yl * 4 + x_o, t)
    yp = ((1 - yl) * 4 + x, t)
    sib = (dp, yh * 8 + z * 2 + (1 - core))
    zr, zl, zo = ((dp, yh * 8 + q * 2 + core) for q in (z_r, z_l, z_o))
    yhp = (dp, (1 - yh) * 8 + z * 2 + core)
    peers = (xr, xl, xo, yp, sib, zr, zl, zo, yhp)

    weights = [
        pltpu.make_async_copy(wg_hbm, wgu.at[:, pl.ds(0, FL)], wsem.at[0]),
        pltpu.make_async_copy(wu_hbm, wgu.at[:, pl.ds(FL, FL)], wsem.at[1]),
        pltpu.make_async_copy(wd_hbm, wd, wsem.at[2]),
    ]
    for w in weights:
        w.start()

    barrier = pltpu.get_barrier_semaphore()
    for dev in peers:
        pl.semaphore_signal(barrier, inc=1, device_id=dev, device_id_type=pl.DeviceIdType.MESH)

    sent = []

    def remote(src, dst, k, dev):
        return pltpu.make_async_remote_copy(
            src_ref=src, dst_ref=dst, send_sem=ss.at[k], recv_sem=rs.at[k],
            device_id=dev, device_id_type=pl.DeviceIdType.MESH,
        )

    def send(src, dst, k, dev):
        copy = remote(src, dst, k, dev)
        copy.start()
        sent.append(copy)

    def got(dst, k):
        remote(dst, dst, k, sib).wait_recv()

    def row(c, zz, y):
        return pl.multiple_of(((y * 2 + c) * 4 + zz) * ROWS, ROWS)

    def gather(view, part, k):
        def put(v, i, dev):
            send(v, v, k + i, dev)

        def p1():
            own = view(row(core, z, yh))
            put(own, 0, zr)
            put(own, 1, zl)
            put(own, 2, sib)

        def q1():
            put(part(row(core, z, yh), 0), 8, yhp)
            put(part(row(core, z, yh), 1), 9, yhp)

        def p2():
            left, right = row(core, z_l, yh), row(core, z_r, yh)
            got(view(left), k)
            put(part(left, 0), 3, zr)
            got(view(right), k + 1)
            put(part(right, 1), 4, zl)
            put(view(left), 5, sib)
            put(view(right), 6, sib)

        def p3():
            far = row(core, z_o, yh)
            got(part(far, 0), k + 3)
            got(part(far, 1), k + 4)
            put(view(far), 7, sib)

        def p4():
            for i, q in ((2, z), (5, z_l), (6, z_r), (7, z_o)):
                got(view(row(1 - core, q, yh)), k + i)

        def q2():
            other = row(core, z, 1 - yh)
            for i in range(2):
                got(part(other, i), k + 8 + i)
                put(part(other, i), 10 + i, zr)
                put(part(other, i), 12 + i, zl)
            put(view(other), 14, sib)

        def q3():
            left, right = row(core, z_l, 1 - yh), row(core, z_r, 1 - yh)
            got(part(left, 0), k + 10)
            put(part(left, 0), 15, zr)
            got(part(right, 1), k + 13)
            put(part(right, 1), 16, zl)
            got(part(left, 1), k + 11)
            got(part(right, 0), k + 12)
            put(view(left), 17, sib)
            put(view(right), 18, sib)

        def q4():
            far = row(core, z_o, 1 - yh)
            got(part(far, 0), k + 15)
            got(part(far, 1), k + 16)
            put(view(far), 19, sib)

        def q5():
            for i, q in ((14, z), (17, z_l), (18, z_r), (19, z_o)):
                got(view(row(1 - core, q, 1 - yh)), k + i)

        return p1, p2, p3, p4, q1, q2, q3, q4, q5

    def rows_gather(ref, k):
        return gather(
            lambda r: ref.at[pl.ds(r, ROWS), :],
            lambda r, i: ref.at[pl.ds(r, ROWS), pl.ds(i * 2048, 2048)],
            k,
        )

    np1, np2, np3, np4, nq1, nq2, nq3, nq4, nq5 = rows_gather(nrm, K_NRM)
    cp1, cp2, cp3, cp4, cq1, cq2, cq3, cq4, cq5 = rows_gather(cot, K_COT)
    def slow_gather(view, k):
        def put(v, i, dev):
            send(v, v, k + i, dev)

        def t1():
            own = view(row(core, z, yh), ROWS)
            put(own, 4, yhp)
            put(own, 0, zr)
            put(own, 1, zl)
            put(own, 2, zo)

        def t2():
            other = view(row(core, z, 1 - yh), ROWS)
            got(other, k + 4)
            put(other, 5, zr)
            put(other, 6, zl)
            put(other, 7, zo)

        def t3():
            for i, q in enumerate((z_l, z_r, z_o)):
                got(view(row(core, q, yh), ROWS), k + i)
            put(view(row(core, 0, yh), 64), 3, sib)

        def t4():
            for i, q in enumerate((z_l, z_r, z_o)):
                got(view(row(core, q, 1 - yh), ROWS), k + 5 + i)
            put(view(row(core, 0, 1 - yh), 64), 8, sib)

        def t5():
            got(view(row(1 - core, 0, yh), 64), k + 3)
            got(view(row(1 - core, 0, 1 - yh), 64), k + 8)

        return t1, t2, t3, t4, t5

    a1, a2, a3, a4, a5 = slow_gather(
        lambda r, n: sl.at[pl.ds(0, 2), pl.ds(1, 3), pl.ds(r, n), :], K_SLN
    )
    b1, b2, b3, b4, b5 = slow_gather(
        lambda r, n: sl.at[pl.ds(2, 2), :, pl.ds(r, n), :], K_SLC
    )

    def along_x(block, half, k):
        def x1():
            send(block(0), block(3), k, xr)
            send(block(0), block(1), k + 1, xl)

        def x2():
            got(block(3), k)
            send(half(3, 0), half(2, 0), k + 2, xr)
            got(block(1), k + 1)
            send(half(1, 1), half(2, 1), k + 3, xl)

        def x3():
            got(half(2, 0), k + 2)
            got(half(2, 1), k + 3)

        return x1, x2, x3

    groups = (yh, 1 - yh)

    def group(g):
        return pl.ds(pl.multiple_of(groups[g] * GRP, GRP), GRP)

    def group_lanes(plane, s, g):
        return pl.ds(pl.multiple_of((plane * NX + s) * REP + groups[g] * GRP, GRP), GRP)

    def hidden_group(g, k):
        return along_x(
            lambda s: hid_t.at[:, group_lanes(0, s, g)],
            lambda s, i: hid_t.at[pl.ds(i * 448, 448), group_lanes(0, s, g)],
            k,
        )

    def hidden_partner(at, k):
        def lanes(s):
            return pl.ds((NX + s) * REP, REP)

        return along_x(
            lambda s: hid_t.at[pl.ds(at, 448), lanes(s)],
            lambda s, i: hid_t.at[pl.ds(at + i * 224, 224), lanes(s)],
            k,
        )

    def gate_side(g, at, n, k):
        def rows(s, skip, count):
            return pl.ds(pl.multiple_of(s * REP + groups[g] * GRP + skip, 64), count)

        return along_x(
            lambda s: dgu.at[rows(s, 0, GRP), pl.ds(at, n)],
            lambda s, i: dgu.at[rows(s, i * 64, 64), pl.ds(at, n)],
            k,
        )

    h11, h12, h13 = hidden_group(0, K_H1)
    h21, h22, h23 = hidden_group(1, K_H2)
    pa1, pa2, pa3 = hidden_partner(0, K_PA)
    pb1, pb2, pb3 = hidden_partner(448, K_PB)
    u1, u2, u3 = gate_side(0, FL, FL, K_U1)
    ua1, ua2, ua3 = gate_side(1, FL, WA, K_UA)
    ub1, ub2, ub3 = gate_side(1, FL + WA, WB, K_UB)
    g1, g2, g3 = gate_side(0, 0, FL, K_G1)
    ga1, ga2, ga3 = gate_side(1, 0, WA, K_GA)
    gb1, gb2, gb3 = gate_side(1, WA, WB, K_GB)

    def reduce(part, by_core, by_z, z_sum, by_y, k):
        def r1():
            send(part.at[:, 1 - core], by_core, k, sib)

        def r2():
            got(by_core, k)
            for y in range(2):
                for i in range(2):
                    at = pl.ds(i * 32, 32)
                    part[y, core, at, :] = (
                        part[y, core, at, :].astype(F32) + by_core[y, at, :].astype(F32)
                    ).astype(BF)
            for i, (q, dev) in enumerate(((z_r, zr), (z_l, zl), (z_o, zo))):
                at = pl.ds(pl.multiple_of(q * ROWS, ROWS), ROWS)
                send(part.at[:, core, at, :], by_z.at[i], k + 1 + i, dev)

        def r3():
            for i in range(3):
                got(by_z.at[i], k + 1 + i)
            at = pl.ds(pl.multiple_of(z * ROWS, ROWS), ROWS)
            for y in range(2):
                z_sum[y] = (
                    part[y, core, at, :].astype(F32)
                    + by_z[0, y].astype(F32)
                    + by_z[1, y].astype(F32)
                    + by_z[2, y].astype(F32)
                ).astype(BF)
            send(z_sum.at[1 - yh], by_y, k + 4, yhp)

        def r4():
            got(by_y, k + 4)
            return z_sum[yh].astype(F32) + by_y[...].astype(F32)

        return r1, r2, r3, r4

    o1, o2, o3, o4 = reduce(lo_part, lo_sib, lo_z, lo_zs, lo_y, K_OUT)
    d1, d2, d3, d4 = reduce(dn_part, dn_sib, dn_z, dn_zs, dn_y, K_DNM)

    own = pl.ds(row(core, z, yh), ROWS)
    tokens = tok[...].astype(F32)
    rscale = lax.rsqrt(jnp.mean(tokens * tokens, axis=-1, keepdims=True) + 1e-5)
    gains = gain[...].reshape(1, D).astype(F32)
    nrm[own, :] = (tokens * rscale * gains).astype(BF)
    cot[own, :] = cot_in[...]

    pl.semaphore_wait(barrier, len(peers))
    np1()
    nq1()
    for q in range(NX):
        osl[q, 0] = nrm[own, pl.ds(q * HALF, HALF)]
        osl[q, 1] = nrm[own, pl.ds(2048 + q * HALF, HALF)]
        osl[q, 2] = cot_in[:, pl.ds(pl.multiple_of(yl * 2048 + q * HALF, HALF), HALF)]
    np2()
    cp1()
    nq2()
    cq1()
    send(cot_in.at[:, pl.ds(pl.multiple_of((1 - yl) * 2048, 2048), 2048)], cut, K_CUT, yp)
    np3()
    weights[0].wait()
    weights[1].wait()
    np4()

    def gate_up(g):
        def tile(i):
            at = pl.ds(pl.multiple_of(i * 256, 256), 256)
            gu32[group(g), at] = dot(nrm[group(g), :], wgu[:, at])

        return tile

    def make_hidden(g):
        @pl.loop(0, GRP // 32)
        def _(i):
            at = pl.ds(pl.multiple_of(groups[g] * GRP + i * 32, 32), 32)
            gate, up = gu32[at, pl.ds(0, FL)], gu32[at, pl.ds(FL, FL)]
            hid[at, :] = (gate * jax.nn.sigmoid(gate) * up).astype(BF)

        hid_t[:, group_lanes(0, 0, g)] = hid[group(g), :].T

    def hidden_to_pair(g, k):
        send(hid_t.at[:, group_lanes(0, 0, g)], hid_t.at[:, group_lanes(1, 0, g)], k, yp)

    def make_grads(g):
        rows = group(g)

        def tile(at, n):
            dh = dot_t(cot[rows, :], wd[pl.ds(at, n), :])
            lanes, past = pl.ds(at, n), pl.ds(pl.multiple_of(FL + at, 128), n)
            gate, up = gu32[rows, lanes], gu32[rows, past]
            sig = jax.nn.sigmoid(gate)
            dgu[rows, lanes] = (dh * up * sig * (1.0 + gate * (1.0 - sig))).astype(BF)
            dgu[rows, past] = (dh * (gate * sig)).astype(BF)

        @pl.loop(0, 3)
        def _(i):
            tile(pl.multiple_of(i * 256, 256), 256)

        tile(768, 128)

    pl.loop(0, 3)(gate_up(0))
    cp2()
    nq3()
    got(cut, K_CUT)
    for q in range(NX):
        osl[q, 3] = cut[:, pl.ds(q * HALF, HALF)]
    for i, (q, dev, slot) in enumerate(((x_r, xr, 3), (x_l, xl, 1), (x_o, xo, 2))):
        send(osl.at[q], sl.at[:, slot, own, :], K_A2A + i, dev)
    for i in range(2, 4):
        sl[i, 0, own, :] = osl[x, i]
    pl.loop(3, 7)(gate_up(0))
    cp3()
    cq2()
    make_hidden(0)
    h11()
    hidden_to_pair(0, K_HY1)
    nq4()
    cp4()
    weights[2].wait()
    make_grads(0)
    u1()
    for i, slot in enumerate((3, 1, 2)):
        got(sl.at[:, slot, own, :], K_A2A + i)
    cq3()
    a1()
    nq5()
    h12()
    pl.loop(0, 4)(gate_up(1))
    cq4()
    a2()
    b1()
    pl.loop(4, 7)(gate_up(1))
    u2()
    make_hidden(1)
    hidden_to_pair(1, K_HY2)
    cq5()
    make_grads(1)
    ua1()
    ub1()
    a3()
    a4()

    def layer_tile(i):
        at = pl.ds(pl.multiple_of(i * 512, 512), 512)
        lo_part[:, :, :, at] = dot(hid[...], wd[:, at]).astype(BF).reshape(2, 2, 64, 512)

    def normed_tile(i):
        at = pl.ds(pl.multiple_of(i * 512, 512), 512)
        dn_part[:, :, :, at] = (
            dot_t(dgu[pl.ds(0, REP), :], wgu[at, :]).astype(BF).reshape(2, 2, 64, 512)
        )

    pl.loop(0, 8)(layer_tile)
    o1()
    ua2()
    ub2()
    g1()

    for j in range(2):
        lanes = pl.ds(pl.multiple_of(j * 2048 + x * HALF, HALF), HALF)
        nrm_t[pl.ds(j * HALF, HALF), pl.ds(0, REP)] = nrm[:, lanes].T

    a5()

    @pl.loop(1, NX)
    def _(r):
        at = pl.ds(pl.multiple_of(r * REP, REP), REP)
        nrm_t[pl.ds(0, HALF), at] = sl[0, r].T
        nrm_t[pl.ds(HALF, HALF), at] = sl[1, r].T

    def halves(which):
        return pl.ds(pl.multiple_of(which * HALF, HALF), HALF)

    def side(which, at, n):
        return dot(nrm_t[halves(which), :], dgu[:, pl.ds(at, n)]).astype(BF)

    u3()
    ua3()
    pu_send[:, pl.ds(0, WA)] = side(1 - yl, FL, WA)
    send(pu_send.at[:, pl.ds(0, WA)], pu_recv.at[:, pl.ds(0, WA)], K_YUA, yp)
    ub3()
    pu_send[:, pl.ds(WA, WB)] = side(1 - yl, FL + WA, WB)
    send(pu_send.at[:, pl.ds(WA, WB)], pu_recv.at[:, pl.ds(WA, WB)], K_YUB, yp)
    o2()
    ga1()
    gb1()
    g2()
    b2()
    pl.loop(0, 4)(normed_tile)
    ga2()
    pl.loop(4, 8)(normed_tile)
    d1()
    gb2()
    h21()
    b3()
    g3()
    ga3()
    pg_send[:, pl.ds(0, WA)] = side(1 - yl, 0, WA)
    send(pg_send.at[:, pl.ds(0, WA)], pg_recv.at[:, pl.ds(0, WA)], K_YGA, yp)
    gb3()
    pg_send[:, pl.ds(WA, WB)] = side(1 - yl, WA, WB)
    send(pg_send.at[:, pl.ds(WA, WB)], pg_recv.at[:, pl.ds(WA, WB)], K_YGB, yp)
    d2()
    got(hid_t.at[:, group_lanes(1, 0, 0)], K_HY1)
    got(hid_t.at[:, group_lanes(1, 0, 1)], K_HY2)
    pa1()
    pb1()
    h22()
    b4()
    o3()
    gu_v[...] = side(yl, FL, FL)
    pa2()
    gg_v[...] = side(yl, 0, FL)
    pb2()
    d3()
    b5()

    def down(plane):
        return dot(
            hid_t[:, pl.ds(plane * NX * REP, NX * REP)],
            sl[2 + plane].reshape(NX * REP, HALF),
        )

    h13()
    h23()
    gd_v[...] = down(0).astype(BF)

    out = []

    def leave(v, o, i):
        copy = pltpu.make_async_copy(v, o, osem.at[i])
        copy.start()
        out.append(copy)

    lo_v[...] = (tokens + o4()).astype(BF)
    leave(lo_v, lo_out, 0)
    g = d4() * gains
    xhat = tokens * rscale
    inner = jnp.mean(g * xhat, axis=-1, keepdims=True)
    tig_v[...] = (cot_in[...].astype(F32) + rscale * (g - xhat * inner)).astype(BF)
    leave(tig_v, tig_out, 1)

    def finish(v, recv, at, n, k):
        lanes = pl.ds(at, n)
        got(recv.at[:, lanes], k)
        v[:, lanes] = (v[:, lanes].astype(F32) + recv[:, lanes].astype(F32)).astype(BF)

    finish(gu_v, pu_recv, 0, WA, K_YUA)
    finish(gu_v, pu_recv, WA, WB, K_YUB)
    leave(gu_v, gu_out, 2)
    finish(gg_v, pg_recv, 0, WA, K_YGA)
    pa3()
    pb3()
    gd_v[...] = (gd_v[...].astype(F32) + down(1)).astype(BF)
    leave(gd_v, gd_out, 3)
    finish(gg_v, pg_recv, WA, WB, K_YGB)
    leave(gg_v, gg_out, 4)
    for copy in sent:
        copy.wait_send()
    for copy in out:
        copy.wait()


def move(*refs):
    sources, results, held = refs[:5], refs[5:10], refs[10:15]
    sems_in, sems_out = refs[15:]
    ins = [pltpu.make_async_copy(a, v, sems_in.at[i]) for i, (a, v) in enumerate(zip(sources, held))]
    outs = [pltpu.make_async_copy(v, b, sems_out.at[i]) for i, (v, b) in enumerate(zip(held, results))]
    for copy in ins:
        copy.start()
    for arrived, copy in zip(ins, outs):
        arrived.wait()
        copy.start()
    for copy in outs:
        copy.wait()


def local(tokens, rms_norm_gain, w_gate, w_up, w_down, output_cotangent):
    vmem = pl.BlockSpec(memory_space=pltpu.VMEM)
    hbm = pl.BlockSpec(memory_space=pl.ANY)

    def bf(*shape):
        return pltpu.VMEM(shape, BF)

    shapes = [
        jax.ShapeDtypeStruct((ROWS, D), BF),
        jax.ShapeDtypeStruct((ROWS, D), BF),
        jax.ShapeDtypeStruct((HALF, FL), BF),
        jax.ShapeDtypeStruct((HALF, FL), BF),
        jax.ShapeDtypeStruct((FL, HALF), BF),
    ]
    call = pl.pallas_call(
        kernel,
        out_shape=shapes,
        in_specs=[vmem, vmem, vmem, hbm, hbm, hbm],
        out_specs=[hbm] * 5,
        scratch_shapes=[
            bf(D, 2 * FL), bf(FL, D), bf(REP, D), bf(REP, D),
            bf(4, NX, REP, HALF), bf(NX, 4, ROWS, HALF), bf(ROWS, 2048),
            pltpu.VMEM((REP, 2 * FL), F32),
            bf(REP, FL), bf(FL, 2 * NX * REP), bf(NX * REP, 2 * FL), bf(SL, NX * REP),
            bf(2, 2, 64, D), bf(2, 2, 64, D), bf(2, 64, D), bf(2, 64, D),
            bf(3, 2, ROWS, D), bf(3, 2, ROWS, D), bf(2, ROWS, D), bf(2, ROWS, D), bf(ROWS, D), bf(ROWS, D),
            bf(HALF, FL), bf(HALF, FL), bf(HALF, FL), bf(HALF, FL),
            bf(HALF, FL), bf(HALF, FL), bf(FL, HALF),
            bf(ROWS, D), bf(ROWS, D),
            pltpu.SemaphoreType.DMA((N_SEM,)),
            pltpu.SemaphoreType.DMA((N_SEM,)),
            pltpu.SemaphoreType.DMA((3,)),
            pltpu.SemaphoreType.DMA((5,)),
        ],
        compiler_params=pltpu.CompilerParams(
            collective_id=0, has_side_effects=True, vmem_limit_bytes=63 * 1000 * 1000
        ),
        cost_estimate=pl.CostEstimate(
            flops=18 * REP * D * FL, bytes_accessed=6 * D * FL, transcendentals=2 * REP * FL
        ),
    )
    results = call(tokens, rms_norm_gain, output_cotangent, w_gate, w_up, w_down)
    moved = pl.pallas_call(
        move,
        out_shape=shapes,
        in_specs=[hbm] * 5,
        out_specs=[hbm] * 5,
        scratch_shapes=[pltpu.VMEM(a.shape, BF) for a in shapes]
        + [pltpu.SemaphoreType.DMA((5,)), pltpu.SemaphoreType.DMA((5,))],
    )(*results)
    return tuple(moved)


def solution(mesh):
    placed = (
        P(("dp", "tensor"), None),
        P(),
        P(None, "tensor"),
        P(None, "tensor"),
        P("tensor", None),
        P(("dp", "tensor"), None),
    )
    return jax.shard_map(
        local,
        mesh=mesh,
        in_specs=placed,
        out_specs=(
            P(("dp", "tensor"), None),
            P(("dp", "tensor"), None),
            P("dp", "tensor"),
            P("dp", "tensor"),
            P("tensor", "dp"),
        ),
        check_vma=False,
    )
```

```python
import jax
import jax.numpy as jnp
from jax import lax
from jax.experimental import pallas as pl
from jax.experimental.pallas import tpu as pltpu
from jax.sharding import PartitionSpec as P

BF = jnp.bfloat16
F32 = jnp.float32
ROWS = 16
REP = 256
D = 4096
FL = 896
SL = 1024
HALF = 512
NX = 4

K_NRM, K_COT, K_SLN, K_SLC = 0, 20, 40, 49
K_CUT, K_A2A = 58, 59
K_H1, K_H2, K_PA, K_PB = 62, 66, 70, 74
K_U1, K_UA, K_UB, K_G1, K_GA, K_GB = 78, 82, 86, 90, 94, 98
K_OUT, K_DNM = 102, 107
K_HY1, K_HY2, K_YUA, K_YUB, K_YGA, K_YGB = 112, 113, 114, 115, 116, 117
N_SEM = 118
GRP = 128
WA, WB = 256, 640
VA, VB = 640, 256


def dot(a, b):
    return jnp.dot(a, b, preferred_element_type=F32)


def dot_t(a, b):
    return lax.dot_general(a, b, (((1,), (1,)), ((), ())), preferred_element_type=F32)


def kernel(
    tok, gain, cot_in, wg_hbm, wu_hbm, wd_hbm,
    lo_out, tig_out, gg_out, gu_out, gd_out,
    wgu, wd, nrm, cot, sl, osl, cut, gu32, hid, hid_t, dgu, nrm_t,
    lo_part, dn_part, lo_sib, dn_sib, lo_z, dn_z, lo_zs, dn_zs, lo_y, dn_y,
    pg_send, pu_send, pg_recv, pu_recv,
    gg_v, gu_v, gd_v, lo_v, tig_v,
    ss, rs, wsem, osem,
):
    dp = lax.axis_index("dp")
    t = lax.axis_index("tensor")
    x = lax.rem(dp, 4)
    yl = lax.div(dp, 4)
    core = lax.rem(t, 2)
    z = lax.rem(lax.div(t, 2), 4)
    yh = lax.div(t, 8)
    z_r, z_l, z_o = lax.rem(z + 1, 4), lax.rem(z + 3, 4), lax.rem(z + 2, 4)
    x_r, x_l, x_o = lax.rem(x + 1, 4), lax.rem(x + 3, 4), lax.rem(x + 2, 4)
    xr, xl, xo = (yl * 4 + x_r, t), (yl * 4 + x_l, t), (yl * 4 + x_o, t)
    yp = ((1 - yl) * 4 + x, t)
    sib = (dp, yh * 8 + z * 2 + (1 - core))
    zr, zl, zo = ((dp, yh * 8 + q * 2 + core) for q in (z_r, z_l, z_o))
    yhp = (dp, (1 - yh) * 8 + z * 2 + core)
    peers = (xr, xl, xo, yp, sib, zr, zl, zo, yhp)

    weights = [
        pltpu.make_async_copy(wg_hbm, wgu.at[:, pl.ds(0, FL)], wsem.at[0]),
        pltpu.make_async_copy(wu_hbm, wgu.at[:, pl.ds(FL, FL)], wsem.at[1]),
        pltpu.make_async_copy(wd_hbm, wd, wsem.at[2]),
    ]
    for w in weights:
        w.start()

    barrier = pltpu.get_barrier_semaphore()
    for dev in peers:
        pl.semaphore_signal(barrier, inc=1, device_id=dev, device_id_type=pl.DeviceIdType.MESH)

    sent = []

    def remote(src, dst, k, dev):
        return pltpu.make_async_remote_copy(
            src_ref=src, dst_ref=dst, send_sem=ss.at[k], recv_sem=rs.at[k],
            device_id=dev, device_id_type=pl.DeviceIdType.MESH,
        )

    def send(src, dst, k, dev):
        copy = remote(src, dst, k, dev)
        copy.start()
        sent.append(copy)

    def got(dst, k):
        remote(dst, dst, k, sib).wait_recv()

    def row(c, zz, y):
        return pl.multiple_of(((y * 2 + c) * 4 + zz) * ROWS, ROWS)

    def gather(view, part, k):
        def put(v, i, dev):
            send(v, v, k + i, dev)

        def p1():
            own = view(row(core, z, yh))
            put(own, 0, zr)
            put(own, 1, zl)
            put(own, 2, sib)

        def q1():
            put(part(row(core, z, yh), 0), 8, yhp)
            put(part(row(core, z, yh), 1), 9, yhp)

        def p2():
            left, right = row(core, z_l, yh), row(core, z_r, yh)
            got(view(left), k)
            put(part(left, 0), 3, zr)
            got(view(right), k + 1)
            put(part(right, 1), 4, zl)
            put(view(left), 5, sib)
            put(view(right), 6, sib)

        def p3():
            far = row(core, z_o, yh)
            got(part(far, 0), k + 3)
            got(part(far, 1), k + 4)
            put(view(far), 7, sib)

        def p4():
            for i, q in ((2, z), (5, z_l), (6, z_r), (7, z_o)):
                got(view(row(1 - core, q, yh)), k + i)

        def q2():
            other = row(core, z, 1 - yh)
            for i in range(2):
                got(part(other, i), k + 8 + i)
                put(part(other, i), 10 + i, zr)
                put(part(other, i), 12 + i, zl)
            put(view(other), 14, sib)

        def q3():
            left, right = row(core, z_l, 1 - yh), row(core, z_r, 1 - yh)
            got(part(left, 0), k + 10)
            put(part(left, 0), 15, zr)
            got(part(right, 1), k + 13)
            put(part(right, 1), 16, zl)
            got(part(left, 1), k + 11)
            got(part(right, 0), k + 12)
            put(view(left), 17, sib)
            put(view(right), 18, sib)

        def q4():
            far = row(core, z_o, 1 - yh)
            got(part(far, 0), k + 15)
            got(part(far, 1), k + 16)
            put(view(far), 19, sib)

        def q5():
            for i, q in ((14, z), (17, z_l), (18, z_r), (19, z_o)):
                got(view(row(1 - core, q, 1 - yh)), k + i)

        return p1, p2, p3, p4, q1, q2, q3, q4, q5

    def rows_gather(ref, k):
        return gather(
            lambda r: ref.at[pl.ds(r, ROWS), :],
            lambda r, i: ref.at[pl.ds(r, ROWS), pl.ds(i * 2048, 2048)],
            k,
        )

    np1, np2, np3, np4, nq1, nq2, nq3, nq4, nq5 = rows_gather(nrm, K_NRM)
    cp1, cp2, cp3, cp4, cq1, cq2, cq3, cq4, cq5 = rows_gather(cot, K_COT)
    def slow_gather(view, k):
        def put(v, i, dev):
            send(v, v, k + i, dev)

        def t1():
            own = view(row(core, z, yh), ROWS)
            put(own, 4, yhp)
            put(own, 0, zr)
            put(own, 1, zl)
            put(own, 2, zo)

        def t2():
            other = view(row(core, z, 1 - yh), ROWS)
            got(other, k + 4)
            put(other, 5, zr)
            put(other, 6, zl)
            put(other, 7, zo)

        def t3():
            for i, q in enumerate((z_l, z_r, z_o)):
                got(view(row(core, q, yh), ROWS), k + i)
            put(view(row(core, 0, yh), 64), 3, sib)

        def t4():
            for i, q in enumerate((z_l, z_r, z_o)):
                got(view(row(core, q, 1 - yh), ROWS), k + 5 + i)
            put(view(row(core, 0, 1 - yh), 64), 8, sib)

        def t5():
            got(view(row(1 - core, 0, yh), 64), k + 3)
            got(view(row(1 - core, 0, 1 - yh), 64), k + 8)

        return t1, t2, t3, t4, t5

    a1, a2, a3, a4, a5 = slow_gather(
        lambda r, n: sl.at[pl.ds(0, 2), pl.ds(1, 3), pl.ds(r, n), :], K_SLN
    )
    b1, b2, b3, b4, b5 = slow_gather(
        lambda r, n: sl.at[pl.ds(2, 2), :, pl.ds(r, n), :], K_SLC
    )

    def along_x(block, half, k):
        def x1():
            send(block(0), block(3), k, xr)
            send(block(0), block(1), k + 1, xl)

        def x2():
            got(block(3), k)
            send(half(3, 0), half(2, 0), k + 2, xr)
            got(block(1), k + 1)
            send(half(1, 1), half(2, 1), k + 3, xl)

        def x3():
            got(half(2, 0), k + 2)
            got(half(2, 1), k + 3)

        return x1, x2, x3

    groups = (yh, 1 - yh)

    def group(g):
        return pl.ds(pl.multiple_of(groups[g] * GRP, GRP), GRP)

    def group_lanes(plane, s, g):
        return pl.ds(pl.multiple_of((plane * NX + s) * REP + groups[g] * GRP, GRP), GRP)

    def hidden_group(g, k):
        return along_x(
            lambda s: hid_t.at[:, group_lanes(0, s, g)],
            lambda s, i: hid_t.at[pl.ds(i * 448, 448), group_lanes(0, s, g)],
            k,
        )

    def hidden_partner(at, k):
        def lanes(s):
            return pl.ds((NX + s) * REP, REP)

        return along_x(
            lambda s: hid_t.at[pl.ds(at, 448), lanes(s)],
            lambda s, i: hid_t.at[pl.ds(at + i * 224, 224), lanes(s)],
            k,
        )

    def gate_side(g, at, n, k):
        def rows(s, skip, count):
            return pl.ds(pl.multiple_of(s * REP + groups[g] * GRP + skip, 64), count)

        return along_x(
            lambda s: dgu.at[rows(s, 0, GRP), pl.ds(at, n)],
            lambda s, i: dgu.at[rows(s, i * 64, 64), pl.ds(at, n)],
            k,
        )

    h11, h12, h13 = hidden_group(0, K_H1)
    h21, h22, h23 = hidden_group(1, K_H2)
    pa1, pa2, pa3 = hidden_partner(0, K_PA)
    pb1, pb2, pb3 = hidden_partner(448, K_PB)
    u1, u2, u3 = gate_side(0, FL, FL, K_U1)
    ua1, ua2, ua3 = gate_side(1, FL, WA, K_UA)
    ub1, ub2, ub3 = gate_side(1, FL + WA, WB, K_UB)
    g1, g2, g3 = gate_side(0, 0, FL, K_G1)
    ga1, ga2, ga3 = gate_side(1, 0, VA, K_GA)
    gb1, gb2, gb3 = gate_side(1, VA, VB, K_GB)

    def reduce(part, by_core, by_z, z_sum, by_y, k):
        def r1():
            send(part.at[:, 1 - core], by_core, k, sib)

        def r2():
            got(by_core, k)
            for y in range(2):
                for i in range(2):
                    at = pl.ds(i * 32, 32)
                    part[y, core, at, :] = (
                        part[y, core, at, :].astype(F32) + by_core[y, at, :].astype(F32)
                    ).astype(BF)
            for i, (q, dev) in enumerate(((z_r, zr), (z_l, zl), (z_o, zo))):
                at = pl.ds(pl.multiple_of(q * ROWS, ROWS), ROWS)
                send(part.at[:, core, at, :], by_z.at[i], k + 1 + i, dev)

        def r3():
            for i in range(3):
                got(by_z.at[i], k + 1 + i)
            at = pl.ds(pl.multiple_of(z * ROWS, ROWS), ROWS)
            for y in range(2):
                z_sum[y] = (
                    part[y, core, at, :].astype(F32)
                    + by_z[0, y].astype(F32)
                    + by_z[1, y].astype(F32)
                    + by_z[2, y].astype(F32)
                ).astype(BF)
            send(z_sum.at[1 - yh], by_y, k + 4, yhp)

        def r4():
            got(by_y, k + 4)
            return z_sum[yh].astype(F32) + by_y[...].astype(F32)

        return r1, r2, r3, r4

    o1, o2, o3, o4 = reduce(lo_part, lo_sib, lo_z, lo_zs, lo_y, K_OUT)
    d1, d2, d3, d4 = reduce(dn_part, dn_sib, dn_z, dn_zs, dn_y, K_DNM)

    own = pl.ds(row(core, z, yh), ROWS)
    tokens = tok[...].astype(F32)
    rscale = lax.rsqrt(jnp.mean(tokens * tokens, axis=-1, keepdims=True) + 1e-5)
    gains = gain[...].reshape(1, D).astype(F32)
    nrm[own, :] = (tokens * rscale * gains).astype(BF)
    cot[own, :] = cot_in[...]

    pl.semaphore_wait(barrier, len(peers))
    np1()
    nq1()
    for q in range(NX):
        osl[q, 0] = nrm[own, pl.ds(q * HALF, HALF)]
        osl[q, 1] = nrm[own, pl.ds(2048 + q * HALF, HALF)]
        osl[q, 2] = cot_in[:, pl.ds(pl.multiple_of(yl * 2048 + q * HALF, HALF), HALF)]
    np2()
    cp1()
    nq2()
    cq1()
    send(cot_in.at[:, pl.ds(pl.multiple_of((1 - yl) * 2048, 2048), 2048)], cut, K_CUT, yp)
    np3()
    weights[0].wait()
    weights[1].wait()
    np4()

    def gate_up(g):
        def tile(i):
            at = pl.ds(pl.multiple_of(i * 256, 256), 256)
            gu32[group(g), at] = dot(nrm[group(g), :], wgu[:, at])

        return tile

    def make_hidden(g):
        @pl.loop(0, GRP // 32)
        def _(i):
            at = pl.ds(pl.multiple_of(groups[g] * GRP + i * 32, 32), 32)
            gate, up = gu32[at, pl.ds(0, FL)], gu32[at, pl.ds(FL, FL)]
            hid[at, :] = (gate * jax.nn.sigmoid(gate) * up).astype(BF)

        hid_t[:, group_lanes(0, 0, g)] = hid[group(g), :].T

    def hidden_to_pair(g, k):
        send(hid_t.at[:, group_lanes(0, 0, g)], hid_t.at[:, group_lanes(1, 0, g)], k, yp)

    def make_grads(g, between=None):
        rows = group(g)

        def tile(at, n):
            dh = dot_t(cot[rows, :], wd[pl.ds(at, n), :])
            lanes, past = pl.ds(at, n), pl.ds(pl.multiple_of(FL + at, 128), n)
            gate, up = gu32[rows, lanes], gu32[rows, past]
            sig = jax.nn.sigmoid(gate)
            dgu[rows, lanes] = (dh * up * sig * (1.0 + gate * (1.0 - sig))).astype(BF)
            dgu[rows, past] = (dh * (gate * sig)).astype(BF)

        tile(0, 256)
        if between is not None:
            between()

        @pl.loop(1, 3)
        def _(i):
            tile(pl.multiple_of(i * 256, 256), 256)

        tile(768, 128)

    pl.loop(0, 3)(gate_up(0))
    cp2()
    nq3()
    got(cut, K_CUT)
    for q in range(NX):
        osl[q, 3] = cut[:, pl.ds(q * HALF, HALF)]
    for i, (q, dev, slot) in enumerate(((x_r, xr, 3), (x_l, xl, 1), (x_o, xo, 2))):
        send(osl.at[q], sl.at[:, slot, own, :], K_A2A + i, dev)
    for i in range(2, 4):
        sl[i, 0, own, :] = osl[x, i]
    pl.loop(3, 7)(gate_up(0))
    cp3()
    cq2()
    make_hidden(0)
    h11()
    hidden_to_pair(0, K_HY1)
    nq4()
    cp4()
    weights[2].wait()
    make_grads(0)
    u1()
    for i, slot in enumerate((3, 1, 2)):
        got(sl.at[:, slot, own, :], K_A2A + i)
    cq3()
    a1()
    nq5()
    h12()
    pl.loop(0, 4)(gate_up(1))
    cq4()
    a2()
    b1()
    pl.loop(4, 7)(gate_up(1))
    u2()
    make_hidden(1)
    hidden_to_pair(1, K_HY2)
    cq5()
    make_grads(1, ua1)
    ub1()
    a3()
    a4()

    def layer_tile(i):
        at = pl.ds(pl.multiple_of(i * 512, 512), 512)
        lo_part[:, :, :, at] = dot(hid[...], wd[:, at]).astype(BF).reshape(2, 2, 64, 512)

    def normed_tile(i):
        at = pl.ds(pl.multiple_of(i * 512, 512), 512)
        dn_part[:, :, :, at] = (
            dot_t(dgu[pl.ds(0, REP), :], wgu[at, :]).astype(BF).reshape(2, 2, 64, 512)
        )

    pl.loop(0, 8)(layer_tile)
    o1()
    ua2()
    ub2()
    g1()

    for j in range(2):
        lanes = pl.ds(pl.multiple_of(j * 2048 + x * HALF, HALF), HALF)
        nrm_t[pl.ds(j * HALF, HALF), pl.ds(0, REP)] = nrm[:, lanes].T

    a5()

    @pl.loop(1, NX)
    def _(r):
        at = pl.ds(pl.multiple_of(r * REP, REP), REP)
        nrm_t[pl.ds(0, HALF), at] = sl[0, r].T
        nrm_t[pl.ds(HALF, HALF), at] = sl[1, r].T

    def halves(which):
        return pl.ds(pl.multiple_of(which * HALF, HALF), HALF)

    def side(which, at, n):
        return dot(nrm_t[halves(which), :], dgu[:, pl.ds(at, n)]).astype(BF)

    u3()
    ua3()
    pu_send[:, pl.ds(0, WA)] = side(1 - yl, FL, WA)
    send(pu_send.at[:, pl.ds(0, WA)], pu_recv.at[:, pl.ds(0, WA)], K_YUA, yp)
    ub3()
    pu_send[:, pl.ds(WA, WB)] = side(1 - yl, FL + WA, WB)
    send(pu_send.at[:, pl.ds(WA, WB)], pu_recv.at[:, pl.ds(WA, WB)], K_YUB, yp)
    o2()
    ga1()
    gb1()
    g2()
    b2()
    pl.loop(0, 4)(normed_tile)
    ga2()
    pl.loop(4, 8)(normed_tile)
    d1()
    gb2()
    h21()
    got(hid_t.at[:, group_lanes(1, 0, 0)], K_HY1)
    got(hid_t.at[:, group_lanes(1, 0, 1)], K_HY2)
    pa1()
    pb1()
    b3()
    g3()
    ga3()
    o3()
    pg_send[:, pl.ds(0, VA)] = side(1 - yl, 0, VA)
    send(pg_send.at[:, pl.ds(0, VA)], pg_recv.at[:, pl.ds(0, VA)], K_YGA, yp)
    gb3()
    pg_send[:, pl.ds(VA, VB)] = side(1 - yl, VA, VB)
    send(pg_send.at[:, pl.ds(VA, VB)], pg_recv.at[:, pl.ds(VA, VB)], K_YGB, yp)
    d2()
    h22()
    b4()
    gu_v[...] = side(yl, FL, FL)
    pa2()
    gg_v[...] = side(yl, 0, FL)
    pb2()
    d3()
    b5()

    def down(plane):
        return dot(
            hid_t[:, pl.ds(plane * NX * REP, NX * REP)],
            sl[2 + plane].reshape(NX * REP, HALF),
        )

    h13()
    h23()
    gd_v[...] = down(0).astype(BF)

    out = []

    def leave(v, o, i):
        copy = pltpu.make_async_copy(v, o, osem.at[i])
        copy.start()
        out.append(copy)

    def finish(v, recv, at, n, k):
        lanes = pl.ds(at, n)
        got(recv.at[:, lanes], k)
        v[:, lanes] = (v[:, lanes].astype(F32) + recv[:, lanes].astype(F32)).astype(BF)

    finish(gu_v, pu_recv, 0, WA, K_YUA)
    finish(gu_v, pu_recv, WA, WB, K_YUB)
    leave(gu_v, gu_out, 2)
    finish(gg_v, pg_recv, 0, VA, K_YGA)
    pa3()
    pb3()
    gd_v[...] = (gd_v[...].astype(F32) + down(1)).astype(BF)
    leave(gd_v, gd_out, 3)
    lo_v[...] = (tokens + o4()).astype(BF)
    leave(lo_v, lo_out, 0)
    g = d4() * gains
    xhat = tokens * rscale
    inner = jnp.mean(g * xhat, axis=-1, keepdims=True)
    tig_v[...] = (cot_in[...].astype(F32) + rscale * (g - xhat * inner)).astype(BF)
    leave(tig_v, tig_out, 1)

    finish(gg_v, pg_recv, VA, VB, K_YGB)
    leave(gg_v, gg_out, 4)
    for copy in sent:
        copy.wait_send()
    for copy in out:
        copy.wait()


def move(*refs):
    sources, results, held = refs[:5], refs[5:10], refs[10:15]
    sems_in, sems_out = refs[15:]
    ins = [pltpu.make_async_copy(a, v, sems_in.at[i]) for i, (a, v) in enumerate(zip(sources, held))]
    outs = [pltpu.make_async_copy(v, b, sems_out.at[i]) for i, (v, b) in enumerate(zip(held, results))]
    for copy in ins:
        copy.start()
    for arrived, copy in zip(ins, outs):
        arrived.wait()
        copy.start()
    for copy in outs:
        copy.wait()


def local(tokens, rms_norm_gain, w_gate, w_up, w_down, output_cotangent):
    vmem = pl.BlockSpec(memory_space=pltpu.VMEM)
    hbm = pl.BlockSpec(memory_space=pl.ANY)

    def bf(*shape):
        return pltpu.VMEM(shape, BF)

    shapes = [
        jax.ShapeDtypeStruct((ROWS, D), BF),
        jax.ShapeDtypeStruct((ROWS, D), BF),
        jax.ShapeDtypeStruct((HALF, FL), BF),
        jax.ShapeDtypeStruct((HALF, FL), BF),
        jax.ShapeDtypeStruct((FL, HALF), BF),
    ]
    call = pl.pallas_call(
        kernel,
        out_shape=shapes,
        in_specs=[vmem, vmem, vmem, hbm, hbm, hbm],
        out_specs=[hbm] * 5,
        scratch_shapes=[
            bf(D, 2 * FL), bf(FL, D), bf(REP, D), bf(REP, D),
            bf(4, NX, REP, HALF), bf(NX, 4, ROWS, HALF), bf(ROWS, 2048),
            pltpu.VMEM((REP, 2 * FL), F32),
            bf(REP, FL), bf(FL, 2 * NX * REP), bf(NX * REP, 2 * FL), bf(SL, NX * REP),
            bf(2, 2, 64, D), bf(2, 2, 64, D), bf(2, 64, D), bf(2, 64, D),
            bf(3, 2, ROWS, D), bf(3, 2, ROWS, D), bf(2, ROWS, D), bf(2, ROWS, D), bf(ROWS, D), bf(ROWS, D),
            bf(HALF, FL), bf(HALF, FL), bf(HALF, FL), bf(HALF, FL),
            bf(HALF, FL), bf(HALF, FL), bf(FL, HALF),
            bf(ROWS, D), bf(ROWS, D),
            pltpu.SemaphoreType.DMA((N_SEM,)),
            pltpu.SemaphoreType.DMA((N_SEM,)),
            pltpu.SemaphoreType.DMA((3,)),
            pltpu.SemaphoreType.DMA((5,)),
        ],
        compiler_params=pltpu.CompilerParams(
            collective_id=0, has_side_effects=True, vmem_limit_bytes=63 * 1000 * 1000
        ),
        cost_estimate=pl.CostEstimate(
            flops=18 * REP * D * FL, bytes_accessed=6 * D * FL, transcendentals=2 * REP * FL
        ),
    )
    results = call(tokens, rms_norm_gain, output_cotangent, w_gate, w_up, w_down)
    moved = pl.pallas_call(
        move,
        out_shape=shapes,
        in_specs=[hbm] * 5,
        out_specs=[hbm] * 5,
        scratch_shapes=[pltpu.VMEM(a.shape, BF) for a in shapes]
        + [pltpu.SemaphoreType.DMA((5,)), pltpu.SemaphoreType.DMA((5,))],
    )(*results)
    return tuple(moved)


def solution(mesh):
    placed = (
        P(("dp", "tensor"), None),
        P(),
        P(None, "tensor"),
        P(None, "tensor"),
        P("tensor", None),
        P(("dp", "tensor"), None),
    )
    return jax.shard_map(
        local,
        mesh=mesh,
        in_specs=placed,
        out_specs=(
            P(("dp", "tensor"), None),
            P(("dp", "tensor"), None),
            P("dp", "tensor"),
            P("dp", "tensor"),
            P("tensor", "dp"),
        ),
        check_vma=False,
    )
```
